32 devices in a mesh: section: 4 (over y, x), dp: 8 (over z, core).
Axes of the slice: x: 2, y: 2, z: 4, core: 2. Of those that a mesh axis runs over, the one named last changes fastest.
Arguments:
- frames: bfloat16 [2, 512, 4096], P(None, 'dp'), may hold values from -6 to 6
- grad_out: bfloat16 [2, 512, 4096], P(None, 'dp'), may hold values from -6 to 6
- norm_gain: bfloat16 [4, 4096], P('section', 'dp'), may hold values from 0.5 to 1.5
- w_reduce: bfloat16 [4, 4096, 512], P('section', 'dp'), may hold values from -0.09375 to 0.09375
- w_restore: bfloat16 [4, 512, 4096], P('section', None, 'dp'), may hold values from -0.25 to 0.25
Outputs:
- grad_gain: float32 [4, 4096], P('section', 'dp')
- grad_reduce: float32 [4, 4096, 512], P('section', 'dp')
- grad_restore: float32 [4, 512, 4096], P('section', None, 'dp')
The draws below stay inside these ranges and needn't reach their ends.
All inputs are finite; a program needn't handle non-finite values.
Results may differ from the reference program's by a relative error of at most 0.023.
Values may be sent and summed in bfloat16 or wider, within the bound.
A program may use at most 128 MiB of HBM per device.

```python
import jax
import jax.numpy as jnp
from jax import lax

D = 4096
R = 512
POOL = 4
MICRO = 2
TOK_MB = 64
SECTIONS = 4
TOKENS = 512
N_SECTION = 4


def spiked(values, stream_key, source, target, blocks, factor):
    owner, partner = [(jnp.arange(values.shape[position]) // (values.shape[position] // blocks)).reshape([-1 if axis == position else 1 for axis in range(values.ndim)]) for position in (source, target)]
    chosen = jax.random.permutation(stream_key, blocks)[partner]
    strong = (owner == chosen) | (owner == (partner + blocks // 2) % blocks)
    return jnp.where(strong, factor * values, values)


def steps_of(key, dims, cuts, least, top_value):
    factor_of = 1.0
    for position, blocks in cuts:
        heights = jax.random.uniform(jax.random.fold_in(jax.random.fold_in(key, 6), position), (blocks,), jnp.float32, least / len(cuts), top_value / len(cuts))
        factor_of = factor_of * jnp.repeat(jnp.exp(heights), dims[position] // blocks).reshape((-1,) + (1,) * (len(dims) - 1 - position))
    return factor_of


def noise(rng, shape, scale, limit, pieces=(), held_as=jnp.bfloat16):
    result = scale * jax.random.normal(rng, shape, jnp.float32)
    if pieces:
        result = result * steps_of(rng, shape, pieces, -0.22, 0.18)
    return jnp.clip(result, -limit, limit).astype(held_as)


def noise_with(rng, dims, deviation, reach, cuts, heavy, dtype=jnp.bfloat16):
    values = deviation * jax.random.normal(rng, dims, jnp.float32)
    if cuts:
        values = values * steps_of(rng, dims, cuts, -0.22, 0.18)
    return jnp.clip(spiked(values, jax.random.fold_in(rng, 3), *heavy), -reach, reach).astype(dtype)


def setup_inputs(seed: int = 0) -> dict:
    seeds = jax.random.split(jax.random.key(seed), 6)
    return {
        "frames": noise_with(seeds[0], (MICRO, TOKENS, D), 1.0, 6.0, ((1, 8),), (1, 2, 8, 2.0)),
        "grad_out": noise_with(seeds[1], (MICRO, TOKENS, D), 1.0, 6.0, ((1, 8),), (1, 2, 8, 2.0)),
        "norm_gain": jnp.clip(1.0 + 0.1 * jax.random.normal(seeds[2], (SECTIONS, D), jnp.float32), 0.5, 1.5).astype(jnp.bfloat16),
        "w_reduce": noise(seeds[3], (SECTIONS, D, R), D ** -0.5, 0.09375, ((0, 4), (1, 8))),
        "w_restore": noise(seeds[4], (SECTIONS, R, D), R ** -0.5, 0.25, ((0, 4), (2, 8))),
    }


epsilon = 1e-06

def normalize(inputs, gain_row):
    values = inputs.astype(jnp.float32)
    inverse = lax.rsqrt(lax.optimization_barrier(jnp.mean(values * values, axis=-1, keepdims=True)) + epsilon)
    normal = values * inverse
    return (values, inverse, normal, (normal * gain_row.astype(jnp.float32)).astype(jnp.bfloat16))

def section_forward(inputs, gain_row, matrix_reduce, matrix_restore):
    values, inverse, normal, normed = normalize(inputs, gain_row)
    before = jnp.dot(normed, matrix_reduce, preferred_element_type=jnp.float32)
    active = (before * jax.nn.sigmoid(before)).astype(jnp.bfloat16)
    return (values + jnp.dot(active, matrix_restore, preferred_element_type=jnp.float32)).astype(jnp.bfloat16)

def section_backward(inputs, upstream, gain_row, matrix_reduce, matrix_restore):
    values, inverse, normal, normed = normalize(inputs, gain_row)
    before = jnp.dot(normed, matrix_reduce, preferred_element_type=jnp.float32)
    gating = jax.nn.sigmoid(before)
    active = (before * gating).astype(jnp.bfloat16)
    grad_active = lax.dot_general(upstream, matrix_restore, (((1,), (1,)), ((), ())), preferred_element_type=jnp.float32)
    grad_before = (grad_active * gating * (1.0 + before * (1.0 - gating))).astype(jnp.bfloat16)
    grad_normed = lax.dot_general(grad_before, matrix_reduce, (((1,), (1,)), ((), ())), preferred_element_type=jnp.float32)
    gain_term = lax.optimization_barrier(jnp.sum(grad_normed * normal, axis=0))
    grad_normal = grad_normed * gain_row.astype(jnp.float32)
    projected = lax.optimization_barrier(jnp.mean(grad_normal * normal, axis=-1, keepdims=True))
    grad_inputs = (upstream.astype(jnp.float32) + inverse * (grad_normal - normal * projected)).astype(jnp.bfloat16)
    return (grad_inputs, normed, grad_before, active, gain_term)

def smooth(stacked):
    values = stacked.astype(jnp.float32)
    grouped = values.reshape(values.shape[:-2] + (values.shape[-2] // POOL, POOL, values.shape[-1]))
    group_means = lax.optimization_barrier(jnp.mean(grouped, axis=-2, keepdims=True))
    return jnp.broadcast_to(group_means, grouped.shape).reshape(values.shape)

def combine(first, second):
    return (first.astype(jnp.float32) + second.astype(jnp.float32)).astype(jnp.bfloat16)

def grouped_rows(stacked):
    batches, rows, width = stacked.shape
    split = stacked.reshape(batches, rows // TOK_MB, TOK_MB, width)
    return jnp.transpose(split, (1, 0, 2, 3)).reshape(rows // TOK_MB, batches * TOK_MB, width)

def rounded_sum(left_groups, right_groups):
    dims_rows = (((0,), (0,)), ((), ()))

    def add_group(total, pair):
        term = lax.dot_general(pair[0], pair[1], dims_rows, preferred_element_type=jnp.float32)
        return (total + term.astype(jnp.bfloat16).astype(jnp.float32), None)
    start = jnp.zeros((left_groups.shape[2], right_groups.shape[2]), jnp.float32)
    total, unused = lax.scan(add_group, start, (left_groups, right_groups))
    return total

def reference(frames, grad_out, norm_gain, w_reduce, w_restore):
    sections = N_SECTION
    middle = sections // 2
    gain_total = jnp.zeros(norm_gain.shape, jnp.float32)
    saved = [[] for section_index in range(sections)]
    for batch_index in range(MICRO):
        kept_inputs = []
        skip_rows = []
        current = frames[batch_index]
        for section_index in range(sections):
            if section_index < middle:
                inputs = current
            elif section_index == middle:
                inputs = (smooth(skip_rows[middle - 1]) + skip_rows[middle - 1].astype(jnp.float32)).astype(jnp.bfloat16)
            else:
                inputs = combine(current, skip_rows[sections - 1 - section_index])
            kept_inputs.append(inputs)
            current = section_forward(inputs, norm_gain[section_index], w_reduce[section_index], w_restore[section_index])
            if section_index < middle:
                skip_rows.append(current)
        returned = [None] * sections
        for section_index in reversed(range(sections)):
            if section_index == sections - 1:
                upstream = grad_out[batch_index]
            elif section_index >= middle:
                upstream = returned[section_index + 1]
            elif section_index == middle - 1:
                upstream = (smooth(returned[middle]) + returned[middle].astype(jnp.float32)).astype(jnp.bfloat16)
            else:
                upstream = combine(returned[section_index + 1], returned[sections - 1 - section_index])
            grad_inputs, normed, grad_before, active, gain_term = section_backward(kept_inputs[section_index], upstream, norm_gain[section_index], w_reduce[section_index], w_restore[section_index])
            returned[section_index] = grad_inputs
            gain_total = gain_total.at[section_index].add(gain_term)
            saved[section_index].append((normed, grad_before, active, upstream))
    reduce_list = []
    restore_list = []
    for section_index in range(sections):
        normed_all = grouped_rows(jnp.stack([item[0] for item in saved[section_index]]))
        before_all = grouped_rows(jnp.stack([item[1] for item in saved[section_index]]))
        active_all = grouped_rows(jnp.stack([item[2] for item in saved[section_index]]))
        upstream_all = grouped_rows(jnp.stack([item[3] for item in saved[section_index]]))
        reduce_list.append(rounded_sum(normed_all, before_all))
        restore_list.append(rounded_sum(active_all, upstream_all))
    return (gain_total, jnp.stack(reduce_list), jnp.stack(restore_list))
```

```python
import functools

import jax
import jax.numpy as jnp
from jax import lax
from jax.experimental import pallas as pl
from jax.experimental.pallas import tpu as pltpu
from jax.sharding import PartitionSpec as P

POOL = 4
EPSILON = 1e-06
EXTRA = 128
HALF = 64
F32 = jnp.float32
BF16 = jnp.bfloat16


def dot(a, b, ca, cb):
    return lax.dot_general(a, b, (((ca,), (cb,)), ((), ())), preferred_element_type=F32)


def split_lanes(column, rows):
    high = column.astype(BF16).astype(F32)
    low = column - high
    lane = lax.broadcasted_iota(jnp.int32, (rows, EXTRA), 1)
    return jnp.where(lane < HALF, high, low).astype(BF16)


def joined(block, R):
    return block[:, R : R + 1] + block[:, R + HALF : R + HALF + 1]


def kernel(
    S, N, D, frames, grad_out, gain, gain_col, w_reduce, w_restore,
    out_gain, out_reduce, out_restore,
    xs, gs, wr, wt, gains, ns, acts, all_n, all_a, all_g, all_u,
    psend, pland, pfull, qsend, qland, ufull, pmine,
    local_sem, in_send, in_recv, w_send, w_recv, p_send, p_recv, q_send, q_recv,
    o_send, o_recv,
):
    me_s, me_d = lax.axis_index("section"), lax.axis_index("dp")
    T, F = xs.shape[1], xs.shape[2]
    R = w_reduce.shape[1]
    B = T // N
    middle = S // 2
    peers = [lax.rem(me_d + i, N) for i in range(1, N)]
    others = [lax.rem(me_s + i, S) for i in range(1, S)]
    sends = []

    def rows(k, size=B):
        return pl.ds(pl.multiple_of(k * size, size), size)

    def remote(src, dst, send, recv, **device):
        return pltpu.make_async_remote_copy(
            src_ref=src, dst_ref=dst, send_sem=send, recv_sem=recv,
            device_id=device, device_id_type=pl.DeviceIdType.MESH,
        )

    barrier = pltpu.get_barrier_semaphore()
    for k in peers:
        pl.semaphore_signal(barrier, inc=1, device_id={"dp": k}, device_id_type=pl.DeviceIdType.MESH)
    for t in others:
        pl.semaphore_signal(barrier, inc=1, device_id={"section": t}, device_id_type=pl.DeviceIdType.MESH)

    mine = rows(me_d)

    def cols(k):
        return pl.ds(pl.multiple_of(k * F, F), F)

    local = [
        pltpu.make_async_copy(frames.at[rows(me_s), cols(me_d)], xs.at[0, mine], local_sem.at[0]),
        pltpu.make_async_copy(grad_out.at[rows(me_s), cols(me_d)], gs.at[S - 1, mine], local_sem.at[1]),
        pltpu.make_async_copy(w_reduce, wr.at[me_s], local_sem.at[2]),
        pltpu.make_async_copy(w_restore, wt.at[me_s], local_sem.at[3]),
        pltpu.make_async_copy(gain, gains.at[me_s], local_sem.at[4]),
    ]
    for c in local:
        c.start()
    pl.semaphore_wait(barrier, N - 1 + S - 1)

    def weights(which, src, dst, i):
        t = others[i]
        return remote(src, dst.at[me_s], w_send.at[which, i], w_recv.at[which, me_s], section=t)

    frame_copies = [
        remote(frames.at[rows(me_s), cols(k)], xs.at[0, mine], in_send.at[0, i], in_recv.at[0, i], dp=k)
        for i, k in enumerate(peers)
    ]
    for c in frame_copies:
        c.start()
    for i in range(S - 1):
        for which, src, dst in ((0, gain, gains), (1, w_reduce, wr)):
            c = weights(which, src, dst, i)
            c.start()
            sends.append(c)
    for i in range(S - 1):
        c = weights(2, w_restore, wt, i)
        c.start()
        sends.append(c)
    grad_copies = [
        remote(grad_out.at[rows(me_s), cols(k)], gs.at[S - 1, mine], in_send.at[1, i], in_recv.at[1, i], dp=k)
        for i, k in enumerate(peers)
    ]
    for c in grad_copies:
        c.start()
    sends += frame_copies + grad_copies
    for c in local:
        c.wait()
    for c in frame_copies:
        c.wait_recv()

    def weights_here(which, t):
        src, dst = ((gain, gains), (w_reduce, wr), (w_restore, wt))[which]

        @pl.when(me_s != t)
        def _():
            remote(src, dst.at[t], w_send.at[which, 0], w_recv.at[which, t], section=others[0]).wait_recv()

    def scatter(sent, land, send, recv):
        copies = [remote(sent.at[rows(k)], land.at[me_d], send.at[i], recv.at[i], dp=k) for i, k in enumerate(peers)]
        for c in copies:
            c.start()
        land[me_d] = sent[mine]
        sends.extend(copies)
        return copies

    def total(copies, land):
        for c in copies:
            c.wait_recv()
        result = land[0].astype(F32)
        for k in range(1, N):
            result += land[k].astype(F32)
        return result

    def share(full, send, recv):
        copies = [remote(full.at[mine], full.at[mine], send.at[i], recv.at[i], dp=k) for i, k in enumerate(peers)]
        for c in copies:
            c.start()
        sends.extend(copies)
        return copies

    owed = []

    def to_owner(which, src, dst, t):
        spot = rows(me_s, T)

        def copy():
            return remote(src, dst.at[spot], o_send.at[which, t], o_recv.at[which, me_s], section=t)

        @pl.when(me_s != t)
        def _():
            copy().start()

        @pl.when(me_s == t)
        def _():
            dst[spot] = src[...]

        owed.append((t, copy))

    def pooled(block):
        i = lax.broadcasted_iota(jnp.int32, (T, T), 0) >> (POOL.bit_length() - 1)
        j = lax.broadcasted_iota(jnp.int32, (T, T), 1) >> (POOL.bit_length() - 1)
        return dot(jnp.where(i == j, 1.0 / POOL, 0.0).astype(BF16), block, 1, 0)

    def q_scatter(s):
        qsend[s] = dot(gs[s], wt[s], 1, 1).astype(BF16)
        return scatter(qsend.at[s], qland.at[s], q_send.at[s, 0], q_recv.at[s, 0])

    def u_share(s, copies):
        q = total(copies, qland.at[s])
        p = pmine[s]
        gate = jax.nn.sigmoid(p)
        ufull[s, mine] = (q * gate * (1.0 + p * (1.0 - gate))).astype(BF16)
        return share(ufull.at[s], q_send.at[s, 1], q_recv.at[s, 1])

    skips = []
    early = None
    early_share = None
    for s in range(S):
        weights_here(0, s)
        weights_here(1, s)
        x = xs[s].astype(F32)
        part = dot((x * gains[s, 0:1]).astype(BF16), wr[s], 1, 0)
        psend[s, :, :R] = part.astype(BF16)
        psend[s, :, R:] = split_lanes(jnp.sum(x * x, axis=1, keepdims=True), T)
        copies = scatter(psend.at[s], pland.at[s], p_send.at[s, 0], p_recv.at[s, 0])
        if s == S - 1:
            for c in grad_copies:
                c.wait_recv()
            weights_here(2, s)
            early = q_scatter(s)
        block = total(copies, pland.at[s])
        inverse = lax.rsqrt(joined(block, R) / D + EPSILON)
        before = block[:, :R] * inverse
        pmine[s] = before
        pfull[s, mine, :R] = before.astype(BF16)
        pfull[s, mine, R:] = split_lanes(inverse, B)
        copies = share(pfull.at[s], p_send.at[s, 1], p_recv.at[s, 1])
        if s == S - 1:
            early_share = u_share(s, early)
        for c in copies:
            c.wait_recv()
        full = pfull[s].astype(F32)
        p = full[:, :R]
        acts[s] = (p * jax.nn.sigmoid(p)).astype(BF16)
        if s < S - 1:
            weights_here(2, s)
            x = xs[s].astype(F32)
            y = (x + dot(acts[s], wt[s], 1, 0)).astype(BF16)
            if s + 1 < middle:
                xs[s + 1] = y
            elif s + 1 == middle:
                xs[s + 1] = (pooled(y) + y.astype(F32)).astype(BF16)
            else:
                xs[s + 1] = (y.astype(F32) + skips[S - 2 - s][...].astype(F32)).astype(BF16)
            if s < middle:
                skips.append(xs.at[s + 1])
        ns[s] = (xs[s].astype(F32) * joined(full, R)).astype(BF16)
        to_owner(0, ns.at[s], all_n, s)
        to_owner(1, acts.at[s], all_a, s)

    for s in reversed(range(S)):
        if s == S - 1:
            copies = early_share
        else:
            copies = u_share(s, q_scatter(s))
        to_owner(2, gs.at[s], all_g, s)
        for c in copies:
            c.wait_recv()
        to_owner(3, ufull.at[s], all_u, s)
        if s > 0:
            u = ufull[s]
            full = pfull[s].astype(F32)
            shift = jnp.sum(u.astype(F32) * full[:, :R], axis=1, keepdims=True) / D
            inverse = joined(full, R)
            normal = xs[s].astype(F32) * inverse
            m = dot(u, wr[s], 1, 1) * gains[s, 0:1]
            e = (gs[s].astype(F32) + inverse * (m - normal * shift)).astype(BF16)
            if s - 1 >= middle:
                gs[s - 1] = e
            elif s == middle:
                gs[s - 1] = (pooled(e) + e.astype(F32)).astype(BF16)
            else:
                gs[s - 1] = (e.astype(F32) + gs[S - 1 - s].astype(F32)).astype(BF16)

    def arrived(which, src, dst):
        for i in range(1, S):
            remote(
                src, dst.at[rows(others[i - 1], T)], o_send.at[which, 0], o_recv.at[which, others[i - 1]],
                section=others[i - 1],
            ).wait_recv()

    arrived(1, acts.at[0], all_a)
    arrived(2, gs.at[0], all_g)
    out_restore[...] = dot(all_a[...], all_g[...], 0, 0)
    arrived(0, ns.at[0], all_n)
    arrived(3, ufull.at[0], all_u)
    term = dot(all_n[...], all_u[...], 0, 0)
    out_reduce[...] = term * gain_col[...]
    out_gain[...] = lax.dot_general(
        jnp.ones((8, R), F32), term * wr[me_s].astype(F32), (((1,), (1,)), ((), ())),
        precision=lax.Precision.HIGHEST, preferred_element_type=F32,
    )
    for c in sends:
        c.wait_send()
    for t, copy in owed:

        @pl.when(me_s != t)
        def _(copy=copy):
            copy().wait_send()


def solution(mesh):
    S, N = mesh.shape["section"], mesh.shape["dp"]

    def body(frames, grad_out, norm_gain, w_reduce, w_restore):
        D = frames.shape[2]
        F, R = w_reduce.shape[1], w_reduce.shape[2]
        held = frames.shape[0] * frames.shape[1]
        B = held // S
        T = B * N
        vmem = pl.BlockSpec(memory_space=pltpu.VMEM)
        anywhere = pl.BlockSpec(memory_space=pl.ANY)
        dma = pltpu.SemaphoreType.DMA
        out_gain, out_reduce, out_restore = pl.pallas_call(
            functools.partial(kernel, S, N, D),
            out_shape=(
                jax.ShapeDtypeStruct((8, F), F32),
                jax.ShapeDtypeStruct((F, R), F32),
                jax.ShapeDtypeStruct((R, F), F32),
            ),
            in_specs=[anywhere, anywhere, vmem, vmem, anywhere, anywhere],
            out_specs=(vmem, vmem, vmem),
            scratch_shapes=[
                pltpu.VMEM((S, T, F), BF16),
                pltpu.VMEM((S, T, F), BF16),
                pltpu.VMEM((S, F, R), BF16),
                pltpu.VMEM((S, R, F), BF16),
                pltpu.VMEM((S, 8, F), F32),
                pltpu.VMEM((S, T, F), BF16),
                pltpu.VMEM((S, T, R), BF16),
                pltpu.VMEM((S * T, F), BF16),
                pltpu.VMEM((S * T, R), BF16),
                pltpu.VMEM((S * T, F), BF16),
                pltpu.VMEM((S * T, R), BF16),
                pltpu.VMEM((S, T, R + EXTRA), BF16),
                pltpu.VMEM((S, N, B, R + EXTRA), BF16),
                pltpu.VMEM((S, T, R + EXTRA), BF16),
                pltpu.VMEM((S, T, R), BF16),
                pltpu.VMEM((S, N, B, R), BF16),
                pltpu.VMEM((S, T, R), BF16),
                pltpu.VMEM((S, B, R), F32),
                dma((5,)), dma((2, N - 1)), dma((2, N - 1)), dma((3, S - 1)), dma((3, S)),
                dma((S, 2, N - 1)), dma((S, 2, N - 1)), dma((S, 2, N - 1)), dma((S, 2, N - 1)), dma((4, S)), dma((4, S)),
            ],
            compiler_params=pltpu.CompilerParams(
                collective_id=0, has_side_effects=True, vmem_limit_bytes=50 * 1024 * 1024
            ),
        )(
            frames.reshape(held, D),
            grad_out.reshape(held, D),
            jnp.broadcast_to(norm_gain.astype(F32), (8, F)),
            norm_gain.astype(F32).reshape(F, 1),
            w_reduce[0],
            w_restore[0],
        )
        return out_gain[:1], out_reduce[None], out_restore[None]

    in_specs = (
        P(None, "dp", None),
        P(None, "dp", None),
        P("section", "dp"),
        P("section", "dp", None),
        P("section", None, "dp"),
    )
    out_specs = (P("section", "dp"), P("section", "dp", None), P("section", None, "dp"))
    return jax.shard_map(body, mesh=mesh, in_specs=in_specs, out_specs=out_specs, check_vma=False)
```

```python
import functools

import jax
import jax.numpy as jnp
from jax import lax
from jax.experimental import pallas as pl
from jax.experimental.pallas import tpu as pltpu
from jax.sharding import PartitionSpec as P

POOL = 4
EPSILON = 1e-06
EXTRA = 128
HALF = 64
F32 = jnp.float32
BF16 = jnp.bfloat16


def dot(a, b, ca, cb):
    return lax.dot_general(a, b, (((ca,), (cb,)), ((), ())), preferred_element_type=F32)


def split_lanes(column, rows):
    high = column.astype(BF16).astype(F32)
    low = column - high
    lane = lax.broadcasted_iota(jnp.int32, (rows, EXTRA), 1)
    return jnp.where(lane < HALF, high, low).astype(BF16)


def joined(block, R):
    return block[:, R : R + 1] + block[:, R + HALF : R + HALF + 1]


def kernel(
    S, N, D, frames, grad_out, gain, gain_col, w_reduce, w_restore,
    out_gain, out_reduce, out_restore,
    xs, gs, wr, wt, gains, ns, acts, all_n, all_a, all_g, all_u,
    psend, ppair, pland, pfull, qsend, qpair, qland, ufull, pmine,
    local_sem, in_send, in_recv, w_send, w_recv, p_send, p_recv, q_send, q_recv,
    o_send, o_recv,
):
    me_s, me_d = lax.axis_index("section"), lax.axis_index("dp")
    T, F = xs.shape[1], xs.shape[2]
    R = w_reduce.shape[1]
    B = T // N
    middle = S // 2
    peers = [lax.rem(me_d + i, N) for i in range(1, N)]
    others = [lax.rem(me_s + i, S) for i in range(1, S)]
    sends = []

    def rows(k, size=B):
        return pl.ds(pl.multiple_of(k * size, size), size)

    def remote(src, dst, send, recv, **device):
        return pltpu.make_async_remote_copy(
            src_ref=src, dst_ref=dst, send_sem=send, recv_sem=recv,
            device_id=device, device_id_type=pl.DeviceIdType.MESH,
        )

    barrier = pltpu.get_barrier_semaphore()
    for k in peers:
        pl.semaphore_signal(barrier, inc=1, device_id={"dp": k}, device_id_type=pl.DeviceIdType.MESH)
    for t in others:
        pl.semaphore_signal(barrier, inc=1, device_id={"section": t}, device_id_type=pl.DeviceIdType.MESH)

    M = N // 2
    chip, core = lax.div(me_d, 2), lax.rem(me_d, 2)
    partner = me_d + 1 - 2 * core
    mine = rows(core * M + chip)

    def cols(k):
        return pl.ds(pl.multiple_of(k * F, F), F)

    local = [
        pltpu.make_async_copy(frames.at[rows(me_s), cols(me_d)], xs.at[0, mine], local_sem.at[0]),
        pltpu.make_async_copy(grad_out.at[rows(me_s), cols(me_d)], gs.at[S - 1, mine], local_sem.at[1]),
        pltpu.make_async_copy(w_reduce, wr.at[me_s], local_sem.at[2]),
        pltpu.make_async_copy(w_restore, wt.at[me_s], local_sem.at[3]),
        pltpu.make_async_copy(gain, gains.at[me_s], local_sem.at[4]),
    ]
    for c in local:
        c.start()
    pl.semaphore_wait(barrier, N - 1 + S - 1)

    def weights(which, src, dst, i):
        t = others[i]
        return remote(src, dst.at[me_s], w_send.at[which, i], w_recv.at[which, me_s], section=t)

    frame_copies = [
        remote(frames.at[rows(me_s), cols(k)], xs.at[0, mine], in_send.at[0, i], in_recv.at[0, i], dp=k)
        for i, k in enumerate(peers)
    ]
    for c in frame_copies:
        c.start()
    for i in range(S - 1):
        for which, src, dst in ((0, gain, gains), (1, w_reduce, wr)):
            c = weights(which, src, dst, i)
            c.start()
            sends.append(c)
    for i in range(S - 1):
        c = weights(2, w_restore, wt, i)
        c.start()
        sends.append(c)
    grad_copies = [
        remote(grad_out.at[rows(me_s), cols(k)], gs.at[S - 1, mine], in_send.at[1, i], in_recv.at[1, i], dp=k)
        for i, k in enumerate(peers)
    ]
    for c in grad_copies:
        c.start()
    sends += frame_copies + grad_copies
    for c in local:
        c.wait()
    for c in frame_copies:
        c.wait_recv()

    def weights_here(which, t):
        src, dst = ((gain, gains), (w_reduce, wr), (w_restore, wt))[which]

        @pl.when(me_s != t)
        def _():
            remote(src, dst.at[t], w_send.at[which, 0], w_recv.at[which, t], section=others[0]).wait_recv()

    def scatter(sent, pair, send, recv):
        c = remote(sent.at[rows(1 - core, T // 2)], pair, send.at[0], recv.at[0], dp=partner)
        c.start()
        sends.append(c)
        return c

    def spread(copy, sent, pair, land, send, recv):
        copy.wait_recv()
        own = sent[rows(core, T // 2)].astype(F32)
        pair[...] = (own + pair[...].astype(F32)).astype(BF16)
        copies = []
        for i in range(1, M):
            place = lax.rem(chip + i, M)
            c = remote(pair.at[rows(place)], land.at[chip], send.at[i], recv.at[i], dp=2 * place + core)
            c.start()
            copies.append(c)
        land[chip] = pair[rows(chip)]
        sends.extend(copies)
        return copies

    def total(copies, land):
        for c in copies:
            c.wait_recv()
        result = land[0].astype(F32)
        for k in range(1, M):
            result += land[k].astype(F32)
        return result

    def share(full, send, recv):
        copies = []
        for i in range(1, M):
            place = lax.rem(chip + i, M)
            copies.append(remote(full.at[mine], full.at[mine], send.at[i], recv.at[i], dp=2 * place + core))
        passed = []
        for i in range(M):
            block = rows(core * M + lax.rem(chip - i + M, M))
            passed.append(
                remote(full.at[block], full.at[block], send.at[M + i], recv.at[M + i], dp=partner)
            )
        for c in copies + passed[:1]:
            c.start()
        sends.extend(copies + passed)
        return copies, passed

    def gather(shared):
        copies, passed = shared
        for c, onward in zip(copies, passed[1:]):
            c.wait_recv()
            onward.start()
        for c in passed:
            c.wait_recv()

    owed = []

    def to_owner(which, src, dst, t):
        spot = rows(me_s, T)

        def copy():
            return remote(src, dst.at[spot], o_send.at[which, t], o_recv.at[which, me_s], section=t)

        @pl.when(me_s != t)
        def _():
            copy().start()

        @pl.when(me_s == t)
        def _():
            dst[spot] = src[...]

        owed.append((t, copy))

    def pooled(block):
        i = lax.broadcasted_iota(jnp.int32, (T, T), 0) >> (POOL.bit_length() - 1)
        j = lax.broadcasted_iota(jnp.int32, (T, T), 1) >> (POOL.bit_length() - 1)
        return dot(jnp.where(i == j, 1.0 / POOL, 0.0).astype(BF16), block, 1, 0)

    def q_scatter(s):
        qsend[s] = dot(gs[s], wt[s], 1, 1).astype(BF16)
        return scatter(qsend.at[s], qpair.at[s], q_send.at[s, 0], q_recv.at[s, 0])

    def q_spread(s, copy):
        return spread(copy, qsend.at[s], qpair.at[s], qland.at[s], q_send.at[s, 0], q_recv.at[s, 0])

    def u_share(s, copies):
        q = total(copies, qland.at[s])
        p = pmine[s]
        gate = jax.nn.sigmoid(p)
        ufull[s, mine] = (q * gate * (1.0 + p * (1.0 - gate))).astype(BF16)
        return share(ufull.at[s], q_send.at[s, 1], q_recv.at[s, 1])

    skips = []
    early = None
    early_share = None
    for s in range(S):
        weights_here(0, s)
        weights_here(1, s)
        x = xs[s].astype(F32)
        part = dot((x * gains[s, 0:1]).astype(BF16), wr[s], 1, 0)
        psend[s, :, :R] = part.astype(BF16)
        psend[s, :, R:] = split_lanes(jnp.sum(x * x, axis=1, keepdims=True), T)
        copies = scatter(psend.at[s], ppair.at[s], p_send.at[s, 0], p_recv.at[s, 0])
        if s == S - 1:
            for c in grad_copies:
                c.wait_recv()
            weights_here(2, s)
            early = q_scatter(s)
        copies = spread(copies, psend.at[s], ppair.at[s], pland.at[s], p_send.at[s, 0], p_recv.at[s, 0])
        if s == S - 1:
            early = q_spread(s, early)
        block = total(copies, pland.at[s])
        inverse = lax.rsqrt(joined(block, R) / D + EPSILON)
        before = block[:, :R] * inverse
        pmine[s] = before
        pfull[s, mine, :R] = before.astype(BF16)
        pfull[s, mine, R:] = split_lanes(inverse, B)
        copies = share(pfull.at[s], p_send.at[s, 1], p_recv.at[s, 1])
        if s == S - 1:
            early_share = u_share(s, early)
        gather(copies)
        full = pfull[s].astype(F32)
        p = full[:, :R]
        acts[s] = (p * jax.nn.sigmoid(p)).astype(BF16)
        if s < S - 1:
            weights_here(2, s)
            x = xs[s].astype(F32)
            y = (x + dot(acts[s], wt[s], 1, 0)).astype(BF16)
            if s + 1 < middle:
                xs[s + 1] = y
            elif s + 1 == middle:
                xs[s + 1] = (pooled(y) + y.astype(F32)).astype(BF16)
            else:
                xs[s + 1] = (y.astype(F32) + skips[S - 2 - s][...].astype(F32)).astype(BF16)
            if s < middle:
                skips.append(xs.at[s + 1])
        ns[s] = (xs[s].astype(F32) * joined(full, R)).astype(BF16)
        to_owner(0, ns.at[s], all_n, s)
        to_owner(1, acts.at[s], all_a, s)

    for s in reversed(range(S)):
        if s == S - 1:
            copies = early_share
        else:
            copies = u_share(s, q_spread(s, q_scatter(s)))
        to_owner(2, gs.at[s], all_g, s)
        gather(copies)
        to_owner(3, ufull.at[s], all_u, s)
        if s > 0:
            u = ufull[s]
            full = pfull[s].astype(F32)
            shift = jnp.sum(u.astype(F32) * full[:, :R], axis=1, keepdims=True) / D
            inverse = joined(full, R)
            normal = xs[s].astype(F32) * inverse
            m = dot(u, wr[s], 1, 1) * gains[s, 0:1]
            e = (gs[s].astype(F32) + inverse * (m - normal * shift)).astype(BF16)
            if s - 1 >= middle:
                gs[s - 1] = e
            elif s == middle:
                gs[s - 1] = (pooled(e) + e.astype(F32)).astype(BF16)
            else:
                gs[s - 1] = (e.astype(F32) + gs[S - 1 - s].astype(F32)).astype(BF16)

    def arrived(which, src, dst):
        for i in range(1, S):
            remote(
                src, dst.at[rows(others[i - 1], T)], o_send.at[which, 0], o_recv.at[which, others[i - 1]],
                section=others[i - 1],
            ).wait_recv()

    arrived(1, acts.at[0], all_a)
    arrived(2, gs.at[0], all_g)
    out_restore[...] = dot(all_a[...], all_g[...], 0, 0)
    arrived(0, ns.at[0], all_n)
    arrived(3, ufull.at[0], all_u)
    term = dot(all_n[...], all_u[...], 0, 0)
    out_reduce[...] = term * gain_col[...]
    out_gain[...] = lax.dot_general(
        jnp.ones((8, R), F32), term * wr[me_s].astype(F32), (((1,), (1,)), ((), ())),
        precision=lax.Precision.HIGHEST, preferred_element_type=F32,
    )
    for c in sends:
        c.wait_send()
    for t, copy in owed:

        @pl.when(me_s != t)
        def _(copy=copy):
            copy().wait_send()


def solution(mesh):
    S, N = mesh.shape["section"], mesh.shape["dp"]

    def body(frames, grad_out, norm_gain, w_reduce, w_restore):
        D = frames.shape[2]
        F, R = w_reduce.shape[1], w_reduce.shape[2]
        held = frames.shape[0] * frames.shape[1]
        B = held // S
        T = B * N
        vmem = pl.BlockSpec(memory_space=pltpu.VMEM)
        anywhere = pl.BlockSpec(memory_space=pl.ANY)
        dma = pltpu.SemaphoreType.DMA
        out_gain, out_reduce, out_restore = pl.pallas_call(
            functools.partial(kernel, S, N, D),
            out_shape=(
                jax.ShapeDtypeStruct((8, F), F32),
                jax.ShapeDtypeStruct((F, R), F32),
                jax.ShapeDtypeStruct((R, F), F32),
            ),
            in_specs=[anywhere, anywhere, vmem, vmem, anywhere, anywhere],
            out_specs=(vmem, vmem, vmem),
            scratch_shapes=[
                pltpu.VMEM((S, T, F), BF16),
                pltpu.VMEM((S, T, F), BF16),
                pltpu.VMEM((S, F, R), BF16),
                pltpu.VMEM((S, R, F), BF16),
                pltpu.VMEM((S, 8, F), F32),
                pltpu.VMEM((S, T, F), BF16),
                pltpu.VMEM((S, T, R), BF16),
                pltpu.VMEM((S * T, F), BF16),
                pltpu.VMEM((S * T, R), BF16),
                pltpu.VMEM((S * T, F), BF16),
                pltpu.VMEM((S * T, R), BF16),
                pltpu.VMEM((S, T, R + EXTRA), BF16),
                pltpu.VMEM((S, T // 2, R + EXTRA), BF16),
                pltpu.VMEM((S, N // 2, B, R + EXTRA), BF16),
                pltpu.VMEM((S, T, R + EXTRA), BF16),
                pltpu.VMEM((S, T, R), BF16),
                pltpu.VMEM((S, T // 2, R), BF16),
                pltpu.VMEM((S, N // 2, B, R), BF16),
                pltpu.VMEM((S, T, R), BF16),
                pltpu.VMEM((S, B, R), F32),
                dma((5,)), dma((2, N - 1)), dma((2, N - 1)), dma((3, S - 1)), dma((3, S)),
                dma((S, 2, N)), dma((S, 2, N)), dma((S, 2, N)), dma((S, 2, N)), dma((4, S)), dma((4, S)),
            ],
            compiler_params=pltpu.CompilerParams(
                collective_id=0, has_side_effects=True, vmem_limit_bytes=50 * 1024 * 1024
            ),
        )(
            frames.reshape(held, D),
            grad_out.reshape(held, D),
            jnp.broadcast_to(norm_gain.astype(F32), (8, F)),
            norm_gain.astype(F32).reshape(F, 1),
            w_reduce[0],
            w_restore[0],
        )
        return out_gain[:1], out_reduce[None], out_restore[None]

    in_specs = (
        P(None, "dp", None),
        P(None, "dp", None),
        P("section", "dp"),
        P("section", "dp", None),
        P("section", None, "dp"),
    )
    out_specs = (P("section", "dp"), P("section", "dp", None), P("section", None, "dp"))
    return jax.shard_map(body, mesh=mesh, in_specs=in_specs, out_specs=out_specs, check_vma=False)
```

```python
import functools

import jax
import jax.numpy as jnp
from jax import lax
from jax.experimental import pallas as pl
from jax.experimental.pallas import tpu as pltpu
from jax.sharding import PartitionSpec as P

POOL = 4
EPSILON = 1e-06
EXTRA = 128
HALF = 64
F32 = jnp.float32
BF16 = jnp.bfloat16


def dot(a, b, ca, cb):
    return lax.dot_general(a, b, (((ca,), (cb,)), ((), ())), preferred_element_type=F32)


def split_lanes(column, rows):
    high = column.astype(BF16).astype(F32)
    low = column - high
    lane = lax.broadcasted_iota(jnp.int32, (rows, EXTRA), 1)
    return jnp.where(lane < HALF, high, low).astype(BF16)


def joined(block, R):
    return block[:, R : R + 1] + block[:, R + HALF : R + HALF + 1]


def kernel(
    S, N, D, frames, grad_out, gain, gain_col, w_reduce, w_restore,
    out_gain, out_reduce, out_restore,
    xs, gs, wr, wt, gains, ns, acts, all_n, all_a, all_g, all_u,
    psend, ppair, pland, pfull, qsend, qpair, qland, ufull, pmine,
    local_sem, in_send, in_recv, w_send, w_recv, p_send, p_recv, q_send, q_recv,
    o_send, o_recv,
):
    me_s, me_d = lax.axis_index("section"), lax.axis_index("dp")
    T, F = xs.shape[1], xs.shape[2]
    R = w_reduce.shape[1]
    B = T // N
    middle = S // 2
    peers = [lax.rem(me_d + i, N) for i in range(1, N)]
    others = [lax.rem(me_s + i, S) for i in range(1, S)]
    sends = []

    def rows(k, size=B):
        return pl.ds(pl.multiple_of(k * size, size), size)

    def remote(src, dst, send, recv, **device):
        return pltpu.make_async_remote_copy(
            src_ref=src, dst_ref=dst, send_sem=send, recv_sem=recv,
            device_id=device, device_id_type=pl.DeviceIdType.MESH,
        )

    barrier = pltpu.get_barrier_semaphore()
    for k in peers:
        pl.semaphore_signal(barrier, inc=1, device_id={"dp": k}, device_id_type=pl.DeviceIdType.MESH)
    for t in others:
        pl.semaphore_signal(barrier, inc=1, device_id={"section": t}, device_id_type=pl.DeviceIdType.MESH)

    M = N // 2
    chip, core = lax.div(me_d, 2), lax.rem(me_d, 2)
    partner = me_d + 1 - 2 * core
    mine = rows(core * M + chip)

    def cols(k):
        return pl.ds(pl.multiple_of(k * F, F), F)

    local = [
        pltpu.make_async_copy(frames.at[rows(me_s), cols(me_d)], xs.at[0, mine], local_sem.at[0]),
        pltpu.make_async_copy(grad_out.at[rows(me_s), cols(me_d)], gs.at[S - 1, mine], local_sem.at[1]),
        pltpu.make_async_copy(w_reduce, wr.at[me_s], local_sem.at[2]),
        pltpu.make_async_copy(w_restore, wt.at[me_s], local_sem.at[3]),
        pltpu.make_async_copy(gain, gains.at[me_s], local_sem.at[4]),
    ]
    for c in local:
        c.start()
    pl.semaphore_wait(barrier, N - 1 + S - 1)

    def weights(which, src, dst, i):
        t = others[i]
        return remote(src, dst.at[me_s], w_send.at[which, i], w_recv.at[which, me_s], section=t)

    frame_copies = [
        remote(frames.at[rows(me_s), cols(k)], xs.at[0, mine], in_send.at[0, i], in_recv.at[0, i], dp=k)
        for i, k in enumerate(peers)
    ]
    for c in frame_copies:
        c.start()
    first_sends = []
    for i in range(S - 1):
        for which, src, dst in ((0, gain, gains), (1, w_reduce, wr)):
            c = weights(which, src, dst, i)
            c.start()
            first_sends.append(c)
    grad_copies = [
        remote(grad_out.at[rows(me_s), cols(k)], gs.at[S - 1, mine], in_send.at[1, i], in_recv.at[1, i], dp=k)
        for i, k in enumerate(peers)
    ]
    for c in grad_copies:
        c.start()
    sends += frame_copies + grad_copies
    for c in local:
        c.wait()
    for c in first_sends:
        c.wait_send()
    for i in range(S - 1):
        c = weights(2, w_restore, wt, i)
        c.start()
        sends.append(c)
    for c in frame_copies:
        c.wait_recv()

    def weights_here(which, t):
        src, dst = ((gain, gains), (w_reduce, wr), (w_restore, wt))[which]

        @pl.when(me_s != t)
        def _():
            remote(src, dst.at[t], w_send.at[which, 0], w_recv.at[which, t], section=others[0]).wait_recv()

    def scatter(sent, pair, send, recv):
        c = remote(sent.at[rows(1 - core, T // 2)], pair, send.at[0], recv.at[0], dp=partner)
        c.start()
        sends.append(c)
        return c

    def spread(copy, sent, pair, land, send, recv):
        copy.wait_recv()
        own = sent[rows(core, T // 2)].astype(F32)
        pair[...] = (own + pair[...].astype(F32)).astype(BF16)
        copies = []
        for i in range(1, M):
            place = lax.rem(chip + i, M)
            c = remote(pair.at[rows(place)], land.at[chip], send.at[i], recv.at[i], dp=2 * place + core)
            c.start()
            copies.append(c)
        land[chip] = pair[rows(chip)]
        sends.extend(copies)
        return copies

    def total(copies, land):
        for c in copies:
            c.wait_recv()
        result = land[0].astype(F32)
        for k in range(1, M):
            result += land[k].astype(F32)
        return result

    def share(full, send, recv):
        copies = []
        for i in range(1, M):
            place = lax.rem(chip + i, M)
            copies.append(remote(full.at[mine], full.at[mine], send.at[i], recv.at[i], dp=2 * place + core))
        passed = []
        for i in range(M):
            block = rows(core * M + lax.rem(chip - i + M, M))
            passed.append(
                remote(full.at[block], full.at[block], send.at[M + i], recv.at[M + i], dp=partner)
            )
        for c in copies + passed[:1]:
            c.start()
        sends.extend(copies + passed)
        return copies, passed

    def gather(shared):
        copies, passed = shared
        for c, onward in zip(copies, passed[1:]):
            c.wait_recv()
            onward.start()
        for c in passed:
            c.wait_recv()

    owed = []

    def to_owner(which, src, dst, t):
        spot = rows(me_s, T)

        def copy():
            return remote(src, dst.at[spot], o_send.at[which, t], o_recv.at[which, me_s], section=t)

        @pl.when(me_s != t)
        def _():
            copy().start()

        @pl.when(me_s == t)
        def _():
            dst[spot] = src[...]

        owed.append((t, copy))

    def pooled(block):
        i = lax.broadcasted_iota(jnp.int32, (T, T), 0) >> (POOL.bit_length() - 1)
        j = lax.broadcasted_iota(jnp.int32, (T, T), 1) >> (POOL.bit_length() - 1)
        return dot(jnp.where(i == j, 1.0 / POOL, 0.0).astype(BF16), block, 1, 0)

    def q_scatter(s):
        qsend[s] = dot(gs[s], wt[s], 1, 1).astype(BF16)
        return scatter(qsend.at[s], qpair.at[s], q_send.at[s, 0], q_recv.at[s, 0])

    def q_spread(s, copy):
        return spread(copy, qsend.at[s], qpair.at[s], qland.at[s], q_send.at[s, 0], q_recv.at[s, 0])

    def u_share(s, copies):
        q = total(copies, qland.at[s])
        p = pmine[s]
        gate = jax.nn.sigmoid(p)
        ufull[s, mine] = (q * gate * (1.0 + p * (1.0 - gate))).astype(BF16)
        return share(ufull.at[s], q_send.at[s, 1], q_recv.at[s, 1])

    def keep(s):
        ns[s] = (xs[s].astype(F32) * joined(pfull[s].astype(F32), R)).astype(BF16)
        to_owner(0, ns.at[s], all_n, s)
        to_owner(1, acts.at[s], all_a, s)

    skips = []
    early = None
    early_share = None
    for s in range(S):
        weights_here(0, s)
        weights_here(1, s)
        x = xs[s].astype(F32)
        part = dot((x * gains[s, 0:1]).astype(BF16), wr[s], 1, 0)
        psend[s, :, :R] = part.astype(BF16)
        psend[s, :, R:] = split_lanes(jnp.sum(x * x, axis=1, keepdims=True), T)
        copies = scatter(psend.at[s], ppair.at[s], p_send.at[s, 0], p_recv.at[s, 0])
        if s > 0:
            keep(s - 1)
        if s == S - 1:
            for c in grad_copies:
                c.wait_recv()
            weights_here(2, s)
            early = q_scatter(s)
        copies = spread(copies, psend.at[s], ppair.at[s], pland.at[s], p_send.at[s, 0], p_recv.at[s, 0])
        if s == S - 1:
            early = q_spread(s, early)
        block = total(copies, pland.at[s])
        inverse = lax.rsqrt(joined(block, R) / D + EPSILON)
        before = block[:, :R] * inverse
        pmine[s] = before
        pfull[s, mine, :R] = before.astype(BF16)
        pfull[s, mine, R:] = split_lanes(inverse, B)
        copies = share(pfull.at[s], p_send.at[s, 1], p_recv.at[s, 1])
        if s == S - 1:
            early_share = u_share(s, early)
        gather(copies)
        full = pfull[s].astype(F32)
        p = full[:, :R]
        acts[s] = (p * jax.nn.sigmoid(p)).astype(BF16)
        if s < S - 1:
            weights_here(2, s)
            x = xs[s].astype(F32)
            y = (x + dot(acts[s], wt[s], 1, 0)).astype(BF16)
            if s + 1 < middle:
                xs[s + 1] = y
            elif s + 1 == middle:
                xs[s + 1] = (pooled(y) + y.astype(F32)).astype(BF16)
            else:
                xs[s + 1] = (y.astype(F32) + skips[S - 2 - s][...].astype(F32)).astype(BF16)
            if s < middle:
                skips.append(xs.at[s + 1])

    for s in reversed(range(S)):
        if s == S - 1:
            copies = early_share
        else:
            copies = q_scatter(s)
            to_owner(2, gs.at[s], all_g, s)
            if s == S - 2:
                keep(S - 1)
                to_owner(2, gs.at[S - 1], all_g, S - 1)
            copies = u_share(s, q_spread(s, copies))
        gather(copies)
        to_owner(3, ufull.at[s], all_u, s)
        if s > 0:
            u = ufull[s]
            full = pfull[s].astype(F32)
            shift = jnp.sum(u.astype(F32) * full[:, :R], axis=1, keepdims=True) / D
            inverse = joined(full, R)
            normal = xs[s].astype(F32) * inverse
            m = dot(u, wr[s], 1, 1) * gains[s, 0:1]
            e = (gs[s].astype(F32) + inverse * (m - normal * shift)).astype(BF16)
            if s - 1 >= middle:
                gs[s - 1] = e
            elif s == middle:
                gs[s - 1] = (pooled(e) + e.astype(F32)).astype(BF16)
            else:
                gs[s - 1] = (e.astype(F32) + gs[S - 1 - s].astype(F32)).astype(BF16)

    def arrived(which, src, dst):
        for i in range(1, S):
            remote(
                src, dst.at[rows(others[i - 1], T)], o_send.at[which, 0], o_recv.at[which, others[i - 1]],
                section=others[i - 1],
            ).wait_recv()

    arrived(1, acts.at[0], all_a)
    arrived(2, gs.at[0], all_g)
    out_restore[...] = dot(all_a[...], all_g[...], 0, 0)
    arrived(0, ns.at[0], all_n)
    arrived(3, ufull.at[0], all_u)
    term = dot(all_n[...], all_u[...], 0, 0)
    out_reduce[...] = term * gain_col[...]
    out_gain[...] = lax.dot_general(
        jnp.ones((8, R), F32), term * wr[me_s].astype(F32), (((1,), (1,)), ((), ())),
        precision=lax.Precision.HIGHEST, preferred_element_type=F32,
    )
    for c in sends:
        c.wait_send()
    for t, copy in owed:

        @pl.when(me_s != t)
        def _(copy=copy):
            copy().wait_send()


def solution(mesh):
    S, N = mesh.shape["section"], mesh.shape["dp"]

    def body(frames, grad_out, norm_gain, w_reduce, w_restore):
        D = frames.shape[2]
        F, R = w_reduce.shape[1], w_reduce.shape[2]
        held = frames.shape[0] * frames.shape[1]
        B = held // S
        T = B * N
        vmem = pl.BlockSpec(memory_space=pltpu.VMEM)
        anywhere = pl.BlockSpec(memory_space=pl.ANY)
        dma = pltpu.SemaphoreType.DMA
        out_gain, out_reduce, out_restore = pl.pallas_call(
            functools.partial(kernel, S, N, D),
            out_shape=(
                jax.ShapeDtypeStruct((8, F), F32),
                jax.ShapeDtypeStruct((F, R), F32),
                jax.ShapeDtypeStruct((R, F), F32),
            ),
            in_specs=[anywhere, anywhere, vmem, vmem, anywhere, anywhere],
            out_specs=(vmem, vmem, vmem),
            scratch_shapes=[
                pltpu.VMEM((S, T, F), BF16),
                pltpu.VMEM((S, T, F), BF16),
                pltpu.VMEM((S, F, R), BF16),
                pltpu.VMEM((S, R, F), BF16),
                pltpu.VMEM((S, 8, F), F32),
                pltpu.VMEM((S, T, F), BF16),
                pltpu.VMEM((S, T, R), BF16),
                pltpu.VMEM((S * T, F), BF16),
                pltpu.VMEM((S * T, R), BF16),
                pltpu.VMEM((S * T, F), BF16),
                pltpu.VMEM((S * T, R), BF16),
                pltpu.VMEM((S, T, R + EXTRA), BF16),
                pltpu.VMEM((S, T // 2, R + EXTRA), BF16),
                pltpu.VMEM((S, N // 2, B, R + EXTRA), BF16),
                pltpu.VMEM((S, T, R + EXTRA), BF16),
                pltpu.VMEM((S, T, R), BF16),
                pltpu.VMEM((S, T // 2, R), BF16),
                pltpu.VMEM((S, N // 2, B, R), BF16),
                pltpu.VMEM((S, T, R), BF16),
                pltpu.VMEM((S, B, R), F32),
                dma((5,)), dma((2, N - 1)), dma((2, N - 1)), dma((3, S - 1)), dma((3, S)),
                dma((S, 2, N)), dma((S, 2, N)), dma((S, 2, N)), dma((S, 2, N)), dma((4, S)), dma((4, S)),
            ],
            compiler_params=pltpu.CompilerParams(
                collective_id=0, has_side_effects=True, vmem_limit_bytes=50 * 1024 * 1024
            ),
        )(
            frames.reshape(held, D),
            grad_out.reshape(held, D),
            jnp.broadcast_to(norm_gain.astype(F32), (8, F)),
            norm_gain.astype(F32).reshape(F, 1),
            w_reduce[0],
            w_restore[0],
        )
        return out_gain[:1], out_reduce[None], out_restore[None]

    in_specs = (
        P(None, "dp", None),
        P(None, "dp", None),
        P("section", "dp"),
        P("section", "dp", None),
        P("section", None, "dp"),
    )
    out_specs = (P("section", "dp"), P("section", "dp", None), P("section", None, "dp"))
    return jax.shard_map(body, mesh=mesh, in_specs=in_specs, out_specs=out_specs, check_vma=False)
```
